128 devices in a mesh: ctx: 8 (over x, z_lo), exp: 16 (over z_hi, y, core).
Axes of the slice: x: 4, y: 4, z: 4 (z_hi: 2, z_lo: 2; z = z_hi * 2 + z_lo), core: 2. Of those that a mesh axis runs over, the one named last changes fastest.
Arguments:
- queries: bfloat16 [4, 2048, 4096], P(None, 'ctx', 'exp'), may hold values from -8 to 8
- keys: bfloat16 [4, 2048, 256], P(None, 'ctx'), may hold values from -8 to 8
- values: bfloat16 [4, 2048, 256], P(None, 'ctx'), may hold values from -6 to 6
- residual: bfloat16 [2048, 4, 4096], P(('ctx', 'exp')), may hold values from -6 to 6
- out_weight: bfloat16 [4096, 4096], P('exp'), may hold values from -0.09375 to 0.09375
- norm_gain: float32 [4096], replicated, may hold values from 0.1 to 1.9
- expert_ids: int32 [2048, 4, 8], P(('ctx', 'exp')), may hold values from 0 to 127, all different within a row; in each aligned block of 64 rows (0 to 63, 64 to 127, ..., all dimensions but the last counted through in order) at most 4 rows name the same one
- expert_gates: float32 [2048, 4, 8], P(('ctx', 'exp')), may hold values from 0.2 to 1
- w_gate: bfloat16 [128, 4096, 768], P(('ctx', 'exp')), may hold values from -0.09375 to 0.09375
- w_up: bfloat16 [128, 4096, 768], P(('ctx', 'exp')), may hold values from -0.09375 to 0.09375
- w_down: bfloat16 [128, 768, 4096], P(('ctx', 'exp')), may hold values from -0.21875 to 0.21875
Outputs:
- block_out: bfloat16 [2048, 4, 4096], P(('ctx', 'exp'))
The draws below stay inside these ranges and needn't reach their ends.
Inputs may be any that keep to these rules, and one draw needn't show every extreme that they name: `expert_ids`: each token names 8 different experts; among the 64 tokens of one aligned block no expert is named more than 4 times.
All inputs are finite; a program needn't handle non-finite values.
Results may differ from the reference program's by a relative error of at most 0.025.
Values may be sent and summed in bfloat16 or wider, within the bound.
No kernel may reach another device: no remote copies, remote signals or barrier semaphores. Data moves between devices by JAX's collectives and lax.ppermute only.
A program may use at most 128 MiB of HBM per device.

```python
import math
import jax
import jax.numpy as jnp
import numpy as np
from jax import lax

D = 4096
QUERY_HEAD_COUNT = 32
KEY_VALUE_HEADS = 2
HEAD_SIZE = 128
FFW = 768
TOPK = 8
SEQUENCE_COUNT = 4
SEQUENCE_LENGTH = 2048
EXPERTS = 128
TOK_DEV = 64
CAP = 4
N_CTX = 8
N_EXP = 16


def drawn_pair(key):
    base_key = jax.random.fold_in(key, 31)
    query_key, key_random_seed = jax.random.split(base_key, 2)
    query_vals = jnp.clip(1.4 * jax.random.normal(query_key, (SEQUENCE_COUNT, SEQUENCE_LENGTH, QUERY_HEAD_COUNT * HEAD_SIZE), jnp.float32), -8.0, 8.0)
    key_entries = jnp.clip(1.4 * jax.random.normal(key_random_seed, (SEQUENCE_COUNT, SEQUENCE_LENGTH, KEY_VALUE_HEADS * HEAD_SIZE), jnp.float32), -8.0, 8.0)
    return (query_vals, key_entries)


def draw_queries(key, part):
    return drawn_pair(key)[0].astype(jnp.bfloat16)


def draw_keys(key, part):
    return drawn_pair(key)[1].astype(jnp.bfloat16)


def level_of(key, dims, pieces, smallest, high):
    def one(dim, shards_of):
        draws = jax.random.uniform(jax.random.fold_in(jax.random.fold_in(key, 6), dim), (shards_of,), jnp.float32, smallest / len(pieces), high / len(pieces))
        return jnp.repeat(jnp.exp(draws), dims[dim] // shards_of).reshape((-1,) + (1,) * (len(dims) - dim - 1))

    factor_of = one(*pieces[0])
    for cut in pieces[1:]:
        factor_of = factor_of * one(*cut)
    return factor_of


def shared_out(key, own, number, rows, number_of, top, reach, slope):
    sequence = jax.random.permutation(key, number_of)
    packed, usual = shares(number_of, rows * top, reach, slope, True), shares(number_of, rows * top, reach, slope, False)
    places = jnp.arange(number_of)

    def named(tallies, turn):
        used = int((tallies > 0).sum())
        fixed = max(1, used // 4)
        passed = fixed + (places - fixed + turn * (used - fixed)) % max(1, number_of - fixed)
        return jnp.zeros((number_of,), jnp.int32).at[sequence[jnp.where(places < fixed, places, passed)]].set(jnp.asarray(tallies, jnp.int32))

    tallies = jnp.where(number % 4 == 0, named(packed, number // 4), named(usual, number - number // 4 - 1))
    mixed = jax.random.permutation(jax.random.fold_in(own, 3), number_of)
    donor, sink = mixed[0:number_of // 2 * 2:2], mixed[1:number_of // 2 * 2:2]
    room = jnp.minimum(tallies[donor] - 1, reach - tallies[sink]) // 2
    room = jnp.where((donor == sequence[0]) | (sink == sequence[0]) | (tallies[sink] == 0), 0, jnp.maximum(room, 0))
    passed = jax.random.randint(jax.random.fold_in(own, 4), (number_of // 2,), 0, 1 << 20) % (room + 1)
    tallies = tallies.at[donor].add(-passed).at[sink].add(passed)
    labels = jnp.searchsorted(jnp.cumsum(tallies), jnp.arange(rows * top), side="right").astype(jnp.int32)
    table = labels.reshape(top, rows).T
    table = table[jax.random.permutation(jax.random.fold_in(own, 1), rows)]
    turn = jax.random.randint(jax.random.fold_in(own, 2), (rows, 1), 0, top)
    return jnp.take_along_axis(table, (jnp.arange(top)[None, :] + turn) % top, axis=1)


def shares(amount, total, most, slope, full):
    portions = [(1 << 20) // math.isqrt(standing ** slope) + 1 for standing in range(1, amount + 1)]
    largest = most if full else min(most, max(-(-total // amount), total * portions[0] // sum(portions)))
    least = 1 if total - largest >= amount - 1 else 0
    given, rest = [largest] + [least] * (amount - 1), total - largest - least * (amount - 1)
    while rest > 0:
        candidates = [i for i in range(1, amount) if given[i] < largest] or [i for i in range(1, amount) if given[i] < most]
        pool, left = sum([portions[i] for i in candidates]), rest
        for i in candidates:
            extra = min(most - given[i], max(1, left * portions[i] // pool), rest)
            given[i] = given[i] + extra
            rest = rest - extra
    return np.array(given)


def noise(key, shape, spread, most, cuts=(), held_as=jnp.bfloat16):
    loudness = level_of(key, shape, cuts, -0.22, 0.18) if cuts else 1.0
    drawn = jax.random.normal(key, shape, jnp.float32) * spread * loudness
    return jnp.minimum(jnp.maximum(drawn, -most), most).astype(held_as)


def setup_inputs(seed: int = 0) -> dict:
    seeds = jax.random.split(jax.random.key(seed), 12)
    queries = draw_queries(jax.random.fold_in(seeds[11], 71), 0)
    keys = draw_keys(jax.random.fold_in(seeds[11], 71), 0)
    values = noise(seeds[2], (SEQUENCE_COUNT, SEQUENCE_LENGTH, KEY_VALUE_HEADS * HEAD_SIZE), 1.0, 6.0, ((1, 8),))
    residual = noise(seeds[3], (SEQUENCE_LENGTH, SEQUENCE_COUNT, D), 1.0, 6.0, ((0, 128),))
    out_weight = noise(seeds[4], (QUERY_HEAD_COUNT * HEAD_SIZE, D), (QUERY_HEAD_COUNT * HEAD_SIZE) ** -0.5, 0.09375, ((0, 16),))
    norm_gain = jnp.clip(1.0 + 0.18 * jax.random.normal(seeds[5], (D,), jnp.float32), 0.1, 1.9)
    expert_ids_keys = jax.random.split(jax.random.fold_in(seeds[6], 1), SEQUENCE_LENGTH * SEQUENCE_COUNT // TOK_DEV)
    expert_ids_turns = jax.random.permutation(jax.random.fold_in(seeds[6], 3), SEQUENCE_LENGTH * SEQUENCE_COUNT // TOK_DEV)
    expert_ids = jax.vmap(lambda own, number: shared_out(jax.random.fold_in(seeds[6], 2), own, number, TOK_DEV, EXPERTS, TOPK, CAP, 2))(expert_ids_keys, expert_ids_turns).reshape((SEQUENCE_LENGTH, SEQUENCE_COUNT, TOPK))
    expert_gates = jnp.clip(0.2 + 0.8 * jax.random.uniform(seeds[7], (SEQUENCE_LENGTH, SEQUENCE_COUNT, TOPK), jnp.float32) ** level_of(seeds[7], (SEQUENCE_LENGTH, SEQUENCE_COUNT, TOPK), ((0, 128),), -0.2, 0.2), 0.2, 1.0)
    w_gate = noise(seeds[8], (EXPERTS, D, FFW), D ** -0.5, 0.09375, ((0, 128),))
    w_up = noise(seeds[9], (EXPERTS, D, FFW), D ** -0.5, 0.09375, ((0, 128),))
    w_down = noise(seeds[10], (EXPERTS, FFW, D), FFW ** -0.5, 0.21875, ((0, 128),))
    return dict(queries=queries, keys=keys, values=values, residual=residual, out_weight=out_weight, norm_gain=norm_gain, expert_ids=expert_ids, expert_gates=expert_gates, w_gate=w_gate, w_up=w_up, w_down=w_down)


def head_attention(queries, keys, values):
    group_length = QUERY_HEAD_COUNT // KEY_VALUE_HEADS
    scaling = HEAD_SIZE ** (-0.5)
    positions = jnp.arange(SEQUENCE_LENGTH, dtype=jnp.int32)
    visible = positions[None, :] <= positions[:, None]
    zero_index = jnp.zeros((), jnp.int32)

    def single_head(pair_index):
        seq_index = (pair_index // QUERY_HEAD_COUNT).astype(jnp.int32)
        head_index = (pair_index % QUERY_HEAD_COUNT).astype(jnp.int32)
        kv_index = (head_index // group_length).astype(jnp.int32)
        query_block = lax.dynamic_slice(queries, (seq_index, zero_index, (head_index * HEAD_SIZE).astype(jnp.int32)), (1, SEQUENCE_LENGTH, HEAD_SIZE))[0]
        key_block = lax.dynamic_slice(keys, (seq_index, zero_index, (kv_index * HEAD_SIZE).astype(jnp.int32)), (1, SEQUENCE_LENGTH, HEAD_SIZE))[0]
        value_block = lax.dynamic_slice(values, (seq_index, zero_index, (kv_index * HEAD_SIZE).astype(jnp.int32)), (1, SEQUENCE_LENGTH, HEAD_SIZE))[0]
        scores = jnp.dot(query_block, key_block.T, preferred_element_type=jnp.float32) * scaling
        scores = jnp.where(visible, scores, -jnp.inf)
        row_peak = lax.optimization_barrier(jnp.max(scores, axis=1, keepdims=True))
        weights = jnp.exp(scores - row_peak)
        denom_sum = lax.optimization_barrier(jnp.sum(weights, axis=1, keepdims=True))
        mixed = jnp.dot(weights.astype(jnp.bfloat16), value_block, preferred_element_type=jnp.float32)
        return (mixed / denom_sum).astype(jnp.bfloat16)
    outputs = lax.map(single_head, jnp.arange(SEQUENCE_COUNT * QUERY_HEAD_COUNT, dtype=jnp.int32))
    return outputs.reshape(SEQUENCE_COUNT, QUERY_HEAD_COUNT, SEQUENCE_LENGTH, HEAD_SIZE).transpose(2, 0, 1, 3).reshape(SEQUENCE_LENGTH * SEQUENCE_COUNT, QUERY_HEAD_COUNT * HEAD_SIZE)

def project_heads(attended, out_weight):
    group_width = QUERY_HEAD_COUNT * HEAD_SIZE // N_EXP
    row_count = attended.shape[0]

    def add_group(running, group_index):
        first_col = (group_index * group_width).astype(jnp.int32)
        block_cols = lax.dynamic_slice_in_dim(attended, first_col, group_width, 1)
        weight_rows = lax.dynamic_slice_in_dim(out_weight, first_col, group_width, 0)
        term = jnp.dot(block_cols, weight_rows, preferred_element_type=jnp.float32).astype(jnp.bfloat16)
        term = lax.optimization_barrier(term)
        return (running + term.astype(jnp.float32), None)
    summed, ignored = lax.scan(add_group, jnp.zeros((row_count, D), jnp.float32), jnp.arange(N_EXP, dtype=jnp.int32))
    return summed

def slot_places(flat_ids):
    blocks = N_CTX * N_EXP
    per_block = TOK_DEV * TOPK
    blocked = flat_ids.reshape(blocks, per_block)
    expert_range = jnp.arange(EXPERTS, dtype=jnp.int32)

    def one_block(block_ids):
        onehot = (block_ids[:, None] == expert_range[None, :]).astype(jnp.int32)
        before = jnp.cumsum(onehot, axis=0).astype(jnp.int32) - onehot
        return lax.optimization_barrier(jnp.sum(before * onehot, axis=1)).astype(jnp.int32)
    slots = lax.map(one_block, blocked)
    block_index = jnp.arange(blocks, dtype=jnp.int32)[:, None]
    return (block_index * CAP + slots).reshape(-1).astype(jnp.int32)

def reference(queries, keys, values, residual, out_weight, norm_gain, expert_ids, expert_gates, w_gate, w_up, w_down):
    attended = head_attention(queries, keys, values)
    projected = project_heads(attended, out_weight)
    stream = (residual.reshape(SEQUENCE_LENGTH * SEQUENCE_COUNT, D).astype(jnp.float32) + projected).astype(jnp.bfloat16)
    stream_f = stream.astype(jnp.float32)
    mean_square = lax.optimization_barrier(jnp.mean(stream_f * stream_f, axis=1, keepdims=True))
    normed = (stream_f * lax.rsqrt(mean_square + 1e-06) * norm_gain.astype(jnp.float32)[None, :]).astype(jnp.bfloat16)
    flat_ids = expert_ids.reshape(-1).astype(jnp.int32)
    flat_gates = expert_gates.reshape(-1).astype(jnp.float32)
    places = slot_places(flat_ids)
    pair_count = flat_ids.shape[0]
    pair_index = jnp.arange(pair_count, dtype=jnp.int32)
    table = jnp.zeros((EXPERTS, N_CTX * N_EXP * CAP), jnp.int32).at[flat_ids, places].set(pair_index)
    present = jnp.zeros((EXPERTS, N_CTX * N_EXP * CAP), jnp.float32).at[flat_ids, places].set(1.0)

    def expert_step(running, inputs):
        gate_w, up_w, down_w, members, filled = inputs
        token_rows = (members // TOPK).astype(jnp.int32)
        gathered = normed[token_rows]
        gate_act = jnp.dot(gathered, gate_w, preferred_element_type=jnp.float32)
        up_act = jnp.dot(gathered, up_w, preferred_element_type=jnp.float32)
        expert_hidden = (jax.nn.silu(gate_act) * up_act).astype(jnp.bfloat16)
        expert_out = jnp.dot(expert_hidden, down_w, preferred_element_type=jnp.float32).astype(jnp.bfloat16)
        factor = flat_gates[members] * filled
        return (running.at[token_rows].add(factor[:, None] * expert_out.astype(jnp.float32)), None)
    mixture, ignored = lax.scan(expert_step, jnp.zeros((SEQUENCE_LENGTH * SEQUENCE_COUNT, D), jnp.float32), (w_gate, w_up, w_down, table, present))
    block_out = (stream_f + mixture).astype(jnp.bfloat16)
    return block_out.reshape(SEQUENCE_LENGTH, SEQUENCE_COUNT, D)
```

```python
import jax
import jax.numpy as jnp
from jax import lax
from jax.experimental import pallas as pl
from jax.experimental.pallas import tpu as pltpu
from jax.sharding import Mesh
from jax.sharding import PartitionSpec as P

HEAD = 128
TOPK = 8
CTX = ("x", "zl")
EXP = ("zh", "y", "core")
ALL = CTX + EXP
QUAD = ("zh", "core")
SHAPE = (4, 2, 2, 4, 2)
LOG2E = 1.4426950408889634
F32 = jnp.float32
BF16 = jnp.bfloat16
NEG = -1e30
VMEM = 48 * 1024 * 1024


def nt(a, b):
    return lax.dot_general(a, b, (((1,), (1,)), ((), ())), preferred_element_type=F32)


def tn(a, b):
    return lax.dot_general(a, b, (((0,), (0,)), ((), ())), preferred_element_type=F32)


def attention_kernel(ctx_ref, q_ref, kv_ref, out_ref, top_ref, sum_ref, acc_ref):
    ctx = ctx_ref[0]
    length = q_ref.shape[1]
    rows = 2 * length
    factor = HEAD**-0.5 * LOG2E
    top_ref[...] = jnp.full_like(top_ref, NEG)
    sum_ref[...] = jnp.zeros_like(sum_ref)
    acc_ref[...] = jnp.zeros_like(acc_ref)

    def block(index, masked):
        kv = kv_ref[index]
        for c in range(4):
            g = c // 2
            key = kv[:, g * HEAD : (g + 1) * HEAD]
            value = kv[:, (2 + g) * HEAD : (3 + g) * HEAD]
            query = jnp.concatenate([q_ref[c, :, :HEAD], q_ref[c, :, HEAD:]], axis=0)
            scores = nt(key, query)
            if masked:
                key_pos = lax.broadcasted_iota(jnp.int32, (length, rows), 0)
                query_pos = lax.broadcasted_iota(jnp.int32, (length, rows), 1) % length
                scores = jnp.where(key_pos <= query_pos, scores, NEG)
            old = top_ref[c]
            new = jnp.maximum(old, jnp.max(scores, axis=0, keepdims=True))
            shrink = jnp.exp2((old - new) * factor)
            weights = jnp.exp2((scores - new) * factor)
            sum_ref[c] = sum_ref[c] * shrink + jnp.sum(weights, axis=0, keepdims=True)
            acc_ref[c] = acc_ref[c] * shrink + tn(value, weights.astype(BF16))
            top_ref[c] = new

    block(ctx, True)

    @pl.loop(0, ctx)
    def _(index):
        block(index, False)

    for c in range(4):
        done = (acc_ref[c] / sum_ref[c]).T.astype(BF16)
        out_ref[:, 256 * c : 256 * c + HEAD] = done[:length]
        out_ref[:, 256 * c + HEAD : 256 * (c + 1)] = done[length:]


def attention(ctx, q4, kv):
    length = q4.shape[1]
    return pl.pallas_call(
        attention_kernel,
        out_shape=jax.ShapeDtypeStruct((length, 1024), BF16),
        in_specs=[
            pl.BlockSpec(memory_space=pltpu.SMEM),
            pl.BlockSpec(memory_space=pltpu.VMEM),
            pl.BlockSpec(memory_space=pltpu.VMEM),
        ],
        out_specs=pl.BlockSpec(memory_space=pltpu.VMEM),
        scratch_shapes=[
            pltpu.VMEM((4, 1, 2 * length), F32),
            pltpu.VMEM((4, 1, 2 * length), F32),
            pltpu.VMEM((4, HEAD, 2 * length), F32),
        ],
        compiler_params=pltpu.CompilerParams(vmem_limit_bytes=VMEM),
        name="attention",
    )(ctx, q4, kv)


def project_kernel(att_ref, w0_ref, w1_ref, w2_ref, w3_ref, out_ref):
    total = None
    for c, w_ref in enumerate((w0_ref, w1_ref, w2_ref, w3_ref)):
        part = jnp.dot(
            att_ref[:, 256 * c : 256 * (c + 1)], w_ref[...], preferred_element_type=F32
        )
        total = part if total is None else total + part
    out_ref[...] = total.astype(BF16)


def project(att, weights):
    rows, width = att.shape[0], weights[0].shape[1]
    tile = 1024
    return pl.pallas_call(
        project_kernel,
        grid=(width // tile,),
        out_shape=jax.ShapeDtypeStruct((rows, width), BF16),
        in_specs=[pl.BlockSpec((rows, 1024), lambda i: (0, 0))]
        + [pl.BlockSpec((256, tile), lambda i: (0, i))] * 4,
        out_specs=pl.BlockSpec((rows, tile), lambda i: (0, i)),
        compiler_params=pltpu.CompilerParams(vmem_limit_bytes=VMEM),
        name="project",
    )(att, *weights)


STEPS = 4


def pick(rows, half):
    r = lax.broadcasted_iota(jnp.int32, (rows, 2 * rows), 0)
    c = lax.broadcasted_iota(jnp.int32, (rows, 2 * rows), 1)
    return jnp.where(c == (r // 4) * 8 + 4 * half + r % 4, 1.0, 0.0).astype(BF16)


def expert_kernel(r_ref, wg_ref, wu_ref, wda_ref, wdb_ref, out_ref, gate_ref, up_ref, hid_ref):
    step = pl.program_id(0)
    total = hid_ref.shape[0]
    part = 128

    @pl.when(step == 0)
    def _():
        gate_ref[...] = jnp.zeros_like(gate_ref)
        up_ref[...] = jnp.zeros_like(up_ref)

    @pl.when(step < STEPS)
    def _():
        for half in range(2):
            matrix = pick(part, half)
            x = jnp.concatenate(
                [
                    jnp.dot(
                        matrix,
                        r_ref[2 * part * b : 2 * part * (b + 1), :],
                        preferred_element_type=F32,
                    ).astype(BF16)
                    for b in range(total // part)
                ],
                axis=0,
            )
            gate_ref[...] += jnp.dot(x, wg_ref[half], preferred_element_type=F32)
            up_ref[...] += jnp.dot(x, wu_ref[half], preferred_element_type=F32)

    @pl.when(step == STEPS - 1)
    def _():
        gate = gate_ref[...]
        hid_ref[...] = (gate / (1.0 + jnp.exp(-gate)) * up_ref[...]).astype(BF16)

    @pl.when(step >= STEPS)
    def _():
        hidden = hid_ref[...]
        low = jnp.dot(hidden, wda_ref[...], preferred_element_type=F32).astype(BF16)
        high = jnp.dot(hidden, wdb_ref[...], preferred_element_type=F32).astype(BF16)
        for b in range(total // part):
            rows = slice(part * b, part * (b + 1))
            out_ref[2 * part * b : 2 * part * (b + 1), :] = (
                tn(pick(part, 0), low[rows]) + tn(pick(part, 1), high[rows])
            ).astype(BF16)


def experts(arrived, w_gate, w_up, w_down):
    rows, width = arrived.shape
    hidden = w_down.shape[0]
    tile = width // STEPS
    last = STEPS - 1
    w_in = pl.BlockSpec((2, tile, hidden), lambda i: (0, jnp.minimum(i, last), 0))
    return pl.pallas_call(
        expert_kernel,
        grid=(2 * STEPS,),
        out_shape=jax.ShapeDtypeStruct((rows, width), BF16),
        in_specs=[
            pl.BlockSpec((rows, tile), lambda i: (0, jnp.minimum(i, last))),
            w_in,
            w_in,
            pl.BlockSpec((hidden, tile), lambda i: (0, jnp.maximum(i - STEPS, 0))),
            pl.BlockSpec((hidden, tile), lambda i: (0, jnp.maximum(i - STEPS, 0) + STEPS)),
        ],
        out_specs=pl.BlockSpec((rows, tile), lambda i: (0, jnp.maximum(i - STEPS, 0))),
        scratch_shapes=[
            pltpu.VMEM((rows // 2, hidden), F32),
            pltpu.VMEM((rows // 2, hidden), F32),
            pltpu.VMEM((rows // 2, hidden), BF16),
        ],
        compiler_params=pltpu.CompilerParams(vmem_limit_bytes=VMEM),
        name="experts",
    )(
        arrived,
        w_gate.reshape(2, width, hidden),
        w_up.reshape(2, width, hidden),
        w_down,
        w_down,
    )


def routing(expert_ids, expert_gates, experts_all, capacity):
    positions, sequences, _ = expert_ids.shape
    tokens = positions * sequences
    flat_ids = expert_ids.reshape(-1)
    onehot = (flat_ids[:, None] == jnp.arange(experts_all, dtype=jnp.int32)[None, :]).astype(
        jnp.int32
    )
    before = jnp.cumsum(onehot, axis=0) - onehot
    slot = jnp.sum(before * onehot, axis=1)
    place = (flat_ids * 2 * capacity + slot).reshape(tokens, TOPK)
    rows = jnp.arange(2 * capacity * experts_all, dtype=jnp.int32)
    place_sp = place.reshape(positions, sequences, TOPK).transpose(1, 0, 2).reshape(tokens, TOPK)

    def dispatch_half(half):
        hit = rows[:, None, None] == place_sp[None] + half * capacity
        return jnp.any(hit, axis=2)

    dispatch = jnp.concatenate([dispatch_half(0), dispatch_half(1)], axis=1).astype(BF16)
    gates = expert_gates.reshape(tokens, TOPK)

    def combine_half(half):
        hit = rows[None, None, :] == (place + half * capacity)[:, :, None]
        return jnp.sum(jnp.where(hit, gates[:, :, None], 0.0), axis=1)

    combine = jnp.concatenate([combine_half(0), combine_half(1)], axis=0)
    high = combine.astype(BF16)
    low = (combine - high.astype(F32)).astype(BF16)
    return dispatch, jnp.concatenate([high, low], axis=0)


def local(
    queries,
    keys,
    values,
    residual,
    out_weight,
    norm_gain,
    expert_ids,
    expert_gates,
    w_gate,
    w_up,
    w_down,
):
    ctx_index = lax.axis_index(CTX)
    zh = lax.axis_index("zh")
    quad = lax.axis_index(QUAD)
    quad_count = lax.axis_size(QUAD)
    ctx_count = lax.axis_size(CTX)
    exp_count = lax.axis_size(EXP)
    sequences, length, _ = queries.shape
    width = residual.shape[2]

    key_seq = lax.dynamic_index_in_dim(keys, quad, 0, False)
    value_seq = lax.dynamic_index_in_dim(values, quad, 0, False)

    def ordered(a):
        return jnp.where(zh == 0, a, jnp.concatenate([a[:, HEAD:], a[:, :HEAD]], axis=1))

    kv_mine = jnp.concatenate([ordered(key_seq), ordered(value_seq)], axis=1)
    kv_send = jnp.broadcast_to(kv_mine[None], (ctx_count,) + kv_mine.shape)

    chunks = []
    for s in range(quad_count):
        part = lax.dynamic_index_in_dim(queries, quad ^ s, 0, False)
        if s:
            part = lax.ppermute(part, QUAD, [(i, i ^ s) for i in range(quad_count)])
        chunks.append(part)

    swap = [(0, 1), (1, 0)]
    across = []
    for i in range(4):
        zl, zh_i = i // 2, i % 2
        across.append((i, (1 - zl) * 2 + (1 - zh_i)))
    w_core = lax.ppermute(out_weight, "core", swap)
    w_other = lax.ppermute(out_weight, ("zl", "zh"), across)
    w_both = lax.ppermute(w_other, "core", swap)

    kv = lax.all_to_all(kv_send, CTX, 0, 0, tiled=True)
    attended = attention(ctx_index[None].astype(jnp.int32), jnp.stack(chunks), kv)
    partial_sums = project(attended, (out_weight, w_core, w_other, w_both))
    parts = lax.all_to_all(
        partial_sums.reshape(exp_count, length // exp_count, width), EXP, 0, 0, tiled=True
    )
    positions = length // exp_count
    parts = parts.reshape(2, exp_count // 4, 2, positions, width)
    projected = jnp.sum(parts.astype(F32), axis=1)
    tokens = sequences * positions
    stream = (
        residual.astype(F32).transpose(1, 0, 2) + projected.reshape(sequences, positions, width)
    ).astype(BF16)
    stream = stream.reshape(tokens, width)
    stream_f = stream.astype(F32)
    mean_square = jnp.mean(stream_f * stream_f, axis=1, keepdims=True)
    normed = (stream_f * lax.rsqrt(mean_square + 1e-06) * norm_gain[None, :]).astype(BF16)

    experts_all = w_gate.shape[0] * ctx_count * exp_count
    capacity = tokens * TOPK // experts_all
    dispatch, combine = routing(expert_ids, expert_gates, experts_all, capacity)
    half = width // 2
    halves = jnp.concatenate([normed[:, :half], normed[:, half:]], axis=0)
    outgoing = jnp.dot(dispatch, halves, preferred_element_type=F32).astype(BF16)
    arrived = lax.all_to_all(
        outgoing.reshape(experts_all, 2 * capacity, half), ALL, 0, 0, tiled=True
    )
    produced = experts(
        arrived.reshape(experts_all * 2 * capacity, half), w_gate[0], w_up[0], w_down[0]
    )
    returned = lax.all_to_all(
        produced.reshape(experts_all, 2 * capacity, half), ALL, 0, 0, tiled=True
    )
    mixture = jnp.dot(
        combine, returned.reshape(experts_all * 2 * capacity, half), preferred_element_type=F32
    )
    mixture = mixture[: 2 * tokens] + mixture[2 * tokens :]
    mixture = jnp.concatenate([mixture[:tokens], mixture[tokens:]], axis=1)
    back = stream_f.reshape(sequences, positions, width).transpose(1, 0, 2)
    return (back + mixture.reshape(positions, sequences, width)).astype(BF16)


def solution(mesh):
    fine = Mesh(mesh.devices.reshape(SHAPE), ALL)
    rows = P(ALL, None, None)
    in_specs = (
        P(None, CTX, EXP),
        P(None, CTX, None),
        P(None, CTX, None),
        rows,
        P(EXP, None),
        P(),
        rows,
        rows,
        rows,
        rows,
        rows,
    )
    return jax.shard_map(local, mesh=fine, in_specs=in_specs, out_specs=rows, check_vma=False)
```

```python
import jax
import jax.numpy as jnp
from jax import lax
from jax.experimental import pallas as pl
from jax.experimental.pallas import tpu as pltpu
from jax.sharding import Mesh
from jax.sharding import PartitionSpec as P

HEAD = 128
TOPK = 8
CTX = ("x", "zl")
EXP = ("zh", "yh", "yl", "core")
ALL = CTX + EXP
QUAD = ("yl", "core")
SHAPE = (4, 2, 2, 2, 2, 2)
LOG2E = 1.4426950408889634
F32 = jnp.float32
BF16 = jnp.bfloat16
NEG = -1e30
CHUNKS = 6
VMEM = 40 * 1024 * 1024
VMEM_SMALL = 24 * 1024 * 1024


def cost(microseconds):
    return pl.CostEstimate(
        flops=int(microseconds * 1.1e9), bytes_accessed=1 << 20, transcendentals=0
    )


def nt(a, b):
    return lax.dot_general(a, b, (((1,), (1,)), ((), ())), preferred_element_type=F32)


def tn(a, b):
    return lax.dot_general(a, b, (((0,), (0,)), ((), ())), preferred_element_type=F32)


def attention_kernel(ctx_ref, *refs):
    q_hbm, kv_ref, out_refs = refs[:CHUNKS], refs[CHUNKS], refs[CHUNKS + 1 : CHUNKS + 3]
    q_refs, top_ref, sum_ref, acc_ref, sem = refs[CHUNKS + 3 :]
    loads = [pltpu.make_async_copy(q_hbm[c], q_refs.at[c], sem.at[c]) for c in range(CHUNKS)]
    for load in loads:
        load.start()
    for load in loads:
        load.wait()
    ctx = ctx_ref[0]
    length = kv_ref.shape[1]
    rows = 2 * length
    factor = HEAD**-0.5 * LOG2E

    def block(index, count, first):
        kv = kv_ref[pl.ds(index, count)].reshape(count * length, 2 * HEAD)
        key, value = kv[:, :HEAD], kv[:, HEAD:]
        for c in range(CHUNKS):
            query = jnp.concatenate([q_refs[c, :, :HEAD], q_refs[c, :, HEAD:]], axis=0)
            scores = nt(key, query)
            if first:
                shape = (count * length, rows)
                key_pos = lax.broadcasted_iota(jnp.int32, shape, 0) - (count - 1) * length
                query_pos = lax.broadcasted_iota(jnp.int32, shape, 1) % length
                scores = jnp.where(key_pos <= query_pos, scores, NEG)
            new = jnp.max(scores, axis=0, keepdims=True)
            if not first:
                old = top_ref[c]
                new = jnp.maximum(old, new)
            weights = jnp.exp2((scores - new) * factor)
            total = jnp.sum(weights, axis=0, keepdims=True)
            part = tn(value, weights.astype(BF16))
            if not first:
                shrink = jnp.exp2((old - new) * factor)
                total = total + sum_ref[c] * shrink
                part = part + acc_ref[c] * shrink
            sum_ref[c] = total
            acc_ref[c] = part
            top_ref[c] = new

    @pl.when(ctx % 2 == 1)
    def _():
        block(ctx - 1, 2, True)

    @pl.when(ctx % 2 == 0)
    def _():
        block(ctx, 1, True)

    @pl.loop(0, ctx // 2)
    def _(index):
        block(index * 2, 2, False)

    for c in range(CHUNKS):
        done = (acc_ref[c] / sum_ref[c]).T.astype(BF16)
        out_ref, start = out_refs[c % 2], c // 2 * 256
        out_ref[:, start : start + HEAD] = done[:length]
        out_ref[:, start + HEAD : start + 256] = done[length:]


def attention(ctx, chunks, kv):
    length = kv.shape[1]
    vmem = pl.BlockSpec(memory_space=pltpu.VMEM)
    return pl.pallas_call(
        attention_kernel,
        out_shape=(jax.ShapeDtypeStruct((length, 128 * CHUNKS), BF16),) * 2,
        in_specs=[pl.BlockSpec(memory_space=pltpu.SMEM)]
        + [pl.BlockSpec(memory_space=pl.ANY)] * CHUNKS
        + [vmem],
        out_specs=(vmem, vmem),
        scratch_shapes=[
            pltpu.VMEM((CHUNKS, length, 2 * HEAD), BF16),
            pltpu.VMEM((CHUNKS, 1, 2 * length), F32),
            pltpu.VMEM((CHUNKS, 1, 2 * length), F32),
            pltpu.VMEM((CHUNKS, HEAD, 2 * length), F32),
            pltpu.SemaphoreType.DMA((CHUNKS,)),
        ],
        compiler_params=pltpu.CompilerParams(vmem_limit_bytes=VMEM_SMALL),
        cost_estimate=cost(0.1),
        name="attention",
    )(ctx, *(pltpu.with_memory_space_constraint(q, pltpu.HBM) for q in chunks), kv)


def project_kernel(core_ref, own0_ref, own1_ref, other0_ref, other1_ref, *refs):
    first, second, out_ref = refs[:4], refs[4:8], refs[8]
    core = core_ref[0]
    length = own0_ref.shape[0]
    own_refs, other_refs = (own0_ref, own1_ref), (other0_ref, other1_ref)
    tile = out_ref.shape[3]
    steps = pl.num_programs(0)

    def run(parts):
        total = None
        for c, w_ref in parts:
            rows = jnp.concatenate(
                [
                    own_refs[c % 2][:, 256 * (c // 2) : 256 * (c // 2 + 1)],
                    other_refs[1 - c % 2][:, 256 * (c // 2) : 256 * (c // 2 + 1)],
                ],
                axis=0,
            )
            part = jnp.dot(rows, w_ref[...], preferred_element_type=F32)
            total = part if total is None else total + part
        total = total.astype(BF16)
        out_ref[:, core] = total[:length].reshape(-1, 16, tile)
        out_ref[:, 1 - core] = total[length:].reshape(-1, 16, tile)

    @pl.when(pl.program_id(0) < steps // 2)
    def _():
        run(zip((0, 1, 2, 3), first))

    @pl.when(pl.program_id(0) >= steps // 2)
    def _():
        run(zip((0, 1, 4, 5), second))


def project(core, own, other, first, second):
    rows, width = own[0].shape[0], first[0].shape[1]
    tile = 512
    steps = 2 * width // tile
    att = pl.BlockSpec(own[0].shape, lambda i: (0, 0))
    in_first = pl.BlockSpec((256, tile), lambda i: (0, jnp.minimum(i, steps // 2 - 1)))
    in_second = pl.BlockSpec((256, tile), lambda i: (0, jnp.maximum(i - steps // 2, 0)))
    return pl.pallas_call(
        project_kernel,
        grid=(steps,),
        out_shape=pltpu.HBM((rows // 16, 2, 16, 2 * width), BF16),
        in_specs=[pl.BlockSpec(memory_space=pltpu.SMEM)]
        + [att] * 4
        + [in_first] * 4
        + [in_second] * 4,
        out_specs=pl.BlockSpec((rows // 16, 2, 16, tile), lambda i: (0, 0, 0, i)),
        compiler_params=pltpu.CompilerParams(vmem_limit_bytes=VMEM_SMALL),
        cost_estimate=cost(0.1),
        name="project",
    )(core, *own, *other, *first, *second)


def norm_kernel(parts_ref, res_ref, gain_ref, dispatch_ref, out_ref, stream_ref, x_ref):
    groups, _, _, _, positions, half = parts_ref.shape
    squares = {}
    for s in range(4):
        rows = slice(positions * s, positions * (s + 1))
        total = None
        for h in range(2):
            value = res_ref[h, rows].astype(F32)
            for g in range(groups):
                value = value + parts_ref[g, s // 2, h, s % 2].astype(F32)
            value = value.astype(BF16)
            stream_ref[h, rows] = value
            value = value.astype(F32)
            part = jnp.sum(value * value, axis=1, keepdims=True)
            total = part if total is None else total + part
        squares[s] = lax.rsqrt(total / (2 * half) + 1e-06)
    for s in range(4):
        rows = slice(positions * s, positions * (s + 1))
        for h in range(2):
            value = stream_ref[h, rows].astype(F32) * squares[s] * gain_ref[h]
            x_ref[64 * h + positions * s : 64 * h + positions * (s + 1)] = value.astype(BF16)

    @pl.loop(0, half // 512)
    def _(i):
        cols = pl.ds(pl.multiple_of(i * 512, 512), 512)
        out_ref[:, cols] = jnp.dot(
            dispatch_ref[...], x_ref[:, cols], preferred_element_type=F32
        ).astype(BF16)


def norm_dispatch(parts, held, gain, dispatch):
    half = held.shape[2]
    vmem = pl.BlockSpec(memory_space=pltpu.VMEM)
    return pl.pallas_call(
        norm_kernel,
        out_shape=(
            jax.ShapeDtypeStruct((dispatch.shape[0], half), BF16),
            jax.ShapeDtypeStruct(held.shape, BF16),
        ),
        in_specs=[vmem] * 4,
        out_specs=(vmem, vmem),
        scratch_shapes=[pltpu.VMEM((dispatch.shape[1], half), BF16)],
        compiler_params=pltpu.CompilerParams(vmem_limit_bytes=VMEM_SMALL),
        cost_estimate=cost(2.2),
        name="norm_dispatch",
    )(parts, held, gain, dispatch)


def combine_kernel(ret_ref, combine_ref, stream_ref, out_ref):
    tile = ret_ref.shape[1]
    half = out_ref.shape[1] // 2
    tokens = out_ref.shape[0]
    step = pl.program_id(0)
    mixture = jnp.dot(combine_ref[...], ret_ref[...], preferred_element_type=F32)
    mixture = mixture[: 2 * tokens] + mixture[2 * tokens :]
    to = lax.broadcasted_iota(jnp.int32, (tokens, tokens), 0)
    frm = lax.broadcasted_iota(jnp.int32, (tokens, tokens), 1)
    order = jnp.where(frm == (to % 4) * (tokens // 4) + to // 4, 1.0, 0.0).astype(BF16)
    for h in range(2):
        back = jnp.dot(order, stream_ref[h], preferred_element_type=F32)
        cols = pl.ds(pl.multiple_of(h * half + step * tile, tile), tile)
        out_ref[:, cols] = (back + mixture[tokens * h : tokens * (h + 1)]).astype(BF16)


def combine_rows(returned, combine, stream):
    rows, half = returned.shape
    tokens = stream.shape[1]
    tile = 512
    return pl.pallas_call(
        combine_kernel,
        grid=(half // tile,),
        out_shape=jax.ShapeDtypeStruct((tokens, 2 * half), BF16),
        in_specs=[
            pl.BlockSpec((rows, tile), lambda i: (0, i)),
            pl.BlockSpec(combine.shape, lambda i: (0, 0)),
            pl.BlockSpec((2, tokens, tile), lambda i: (0, 0, i)),
        ],
        out_specs=pl.BlockSpec((tokens, 2 * half), lambda i: (0, 0)),
        compiler_params=pltpu.CompilerParams(vmem_limit_bytes=VMEM_SMALL),
        cost_estimate=cost(4),
        name="combine",
    )(returned, combine, stream)


UP_TILE = 256
DOWN_TILE = 512
BLOCK = 256


def shuffle():
    r = lax.broadcasted_iota(jnp.int32, (BLOCK, BLOCK), 0)
    c = lax.broadcasted_iota(jnp.int32, (BLOCK, BLOCK), 1)
    half, r = r // 128, r % 128
    return jnp.where(c == (r // 4) * 8 + 4 * half + r % 4, 1.0, 0.0).astype(BF16)


def expert_kernel(
    r_ref, wg_hbm, wu_hbm, wd_hbm, out_hbm,
    x_ref, hid_ref, wg_ref, wu_ref, wd_ref, stage_ref, up_sem, down_sem, out_sem,
):
    rows, width = r_ref.shape
    ups = hid_ref.shape[1] // UP_TILE
    loads = []
    for i in range(ups):
        cols = slice(i * UP_TILE, (i + 1) * UP_TILE)
        loads.append(
            (
                pltpu.make_async_copy(wg_hbm.at[:, cols], wg_ref.at[i], up_sem.at[0, i]),
                pltpu.make_async_copy(wu_hbm.at[:, cols], wu_ref.at[i], up_sem.at[1, i]),
            )
        )
        for load in loads[-1]:
            load.start()
    load_down = pltpu.make_async_copy(wd_hbm, wd_ref, down_sem)
    load_down.start()
    matrix = shuffle()

    @pl.loop(0, rows // BLOCK)
    def _(b):
        block = r_ref[pl.ds(pl.multiple_of(b * BLOCK, BLOCK), BLOCK), :]
        moved = jnp.dot(matrix, block, preferred_element_type=F32).astype(BF16)
        to = pl.ds(pl.multiple_of(b * 128, 128), 128)
        x_ref[to, :width] = moved[:128]
        x_ref[to, width:] = moved[128:]

    for i in range(ups):
        for load in loads[i]:
            load.wait()
        x = x_ref[...]
        gate = jnp.dot(x, wg_ref[i], preferred_element_type=F32)
        up = jnp.dot(x, wu_ref[i], preferred_element_type=F32)
        hid_ref[:, i * UP_TILE : (i + 1) * UP_TILE] = (
            gate / (1.0 + jnp.exp(-gate)) * up
        ).astype(BF16)

    load_down.wait()
    stores = []
    for i in range(width // DOWN_TILE):
        cols = slice(i * DOWN_TILE, (i + 1) * DOWN_TILE)
        cols_high = slice(width + i * DOWN_TILE, width + (i + 1) * DOWN_TILE)
        hidden = hid_ref[...]
        low = jnp.dot(hidden, wd_ref[:, cols], preferred_element_type=F32).astype(BF16)
        high = jnp.dot(hidden, wd_ref[:, cols_high], preferred_element_type=F32).astype(BF16)
        for b in range(rows // BLOCK):
            part = slice(128 * b, 128 * (b + 1))
            both = jnp.concatenate([low[part], high[part]], axis=0)
            stage_ref[i, BLOCK * b : BLOCK * (b + 1), :] = tn(matrix, both).astype(BF16)
        store = pltpu.make_async_copy(stage_ref.at[i], out_hbm.at[:, cols], out_sem.at[i])
        store.start()
        stores.append(store)
    for store in stores:
        store.wait()


def experts(arrived, w_gate, w_up, w_down):
    rows, width = arrived.shape
    hidden = w_down.shape[0]
    ups, downs = hidden // UP_TILE, width // DOWN_TILE
    hbm = pl.BlockSpec(memory_space=pl.ANY)
    return pl.pallas_call(
        expert_kernel,
        out_shape=pltpu.HBM((rows, width), BF16),
        in_specs=[pl.BlockSpec(memory_space=pltpu.VMEM)] + [hbm] * 3,
        out_specs=hbm,
        scratch_shapes=[
            pltpu.VMEM((rows // 2, 2 * width), BF16),
            pltpu.VMEM((rows // 2, hidden), BF16),
            pltpu.VMEM((ups, 2 * width, UP_TILE), BF16),
            pltpu.VMEM((ups, 2 * width, UP_TILE), BF16),
            pltpu.VMEM(w_down.shape, BF16),
            pltpu.VMEM((downs, rows, DOWN_TILE), BF16),
            pltpu.SemaphoreType.DMA((2, ups)),
            pltpu.SemaphoreType.DMA,
            pltpu.SemaphoreType.DMA((downs,)),
        ],
        compiler_params=pltpu.CompilerParams(vmem_limit_bytes=VMEM),
        cost_estimate=cost(14),
        name="experts",
    )(
        pltpu.with_memory_space_constraint(arrived, pltpu.VMEM),
        *(pltpu.with_memory_space_constraint(w, pltpu.HBM) for w in (w_gate, w_up, w_down)),
    )


def routing(expert_ids, expert_gates, experts_all, capacity):
    positions, sequences, _ = expert_ids.shape
    tokens = positions * sequences
    flat_ids = expert_ids.reshape(-1)
    onehot = (flat_ids[:, None] == jnp.arange(experts_all, dtype=jnp.int32)[None, :]).astype(
        jnp.int32
    )
    before = jnp.cumsum(onehot, axis=0) - onehot
    slot = jnp.sum(before * onehot, axis=1)
    place = (flat_ids * 2 * capacity + slot).reshape(tokens, TOPK)
    rows = jnp.arange(2 * capacity * experts_all, dtype=jnp.int32)
    place_sp = place.reshape(positions, sequences, TOPK).transpose(1, 0, 2).reshape(tokens, TOPK)

    def dispatch_half(half):
        hit = rows[:, None, None] == place_sp[None] + half * capacity
        return jnp.any(hit, axis=2)

    dispatch = jnp.concatenate([dispatch_half(0), dispatch_half(1)], axis=1).astype(BF16)
    gates = expert_gates.reshape(tokens, TOPK)

    def combine_half(half):
        hit = rows[None, None, :] == (place + half * capacity)[:, :, None]
        return jnp.sum(jnp.where(hit, gates[:, :, None], 0.0), axis=1)

    combine = jnp.concatenate([combine_half(0), combine_half(1)], axis=0)
    high = combine.astype(BF16)
    low = (combine - high.astype(F32)).astype(BF16)
    return dispatch, jnp.concatenate([high, low], axis=0)


def local(
    queries,
    keys,
    values,
    residual,
    out_weight,
    norm_gain,
    expert_ids,
    expert_gates,
    w_gate,
    w_up,
    w_down,
):
    ctx_index = lax.axis_index(CTX)
    zh = lax.axis_index("zh")
    core = lax.axis_index("core")
    quad = lax.axis_index(QUAD)
    quad_count = lax.axis_size(QUAD)
    ctx_count = lax.axis_size(CTX)
    exp_count = lax.axis_size(EXP)
    sequences, length, _ = queries.shape
    width = residual.shape[2]

    def mine(a):
        a = lax.dynamic_index_in_dim(a, quad, 0, False)
        return lax.dynamic_slice_in_dim(a, zh * HEAD, HEAD, 1)

    kv_mine = jnp.concatenate([mine(keys), mine(values)], axis=1)
    kv_send = jnp.broadcast_to(kv_mine[None], (ctx_count,) + kv_mine.shape)

    half = width // 2
    part = half // 2
    ring = ("yh", "yl", "core")
    pairs = {m: [(i, i ^ m) for i in range(8)] for m in range(8)}
    chunks = [lax.dynamic_index_in_dim(queries, quad, 0, False)]
    for m in (1, 2, 3, 6, 7):
        chunk = lax.dynamic_index_in_dim(queries, quad ^ (m & 3), 0, False)
        chunks.append(lax.ppermute(chunk, ring, pairs[m]))

    def columns(of_core, second):
        start = of_core * half + (part if second else 0)
        return lax.dynamic_slice_in_dim(out_weight, start, part, 1)

    mine_a, mine_b, swap_a, swap_b, _ = lax.optimization_barrier(
        (
            columns(core, False),
            columns(core, True),
            columns(1 - core, False),
            columns(1 - core, True),
            chunks[1:],
        )
    )
    first = [mine_a] + [
        lax.ppermute(w, ring, pairs[m]) for w, m in ((swap_a, 1), (mine_a, 2), (swap_a, 3))
    ]
    second = [mine_b] + [
        lax.ppermute(w, ring, pairs[m]) for w, m in ((swap_b, 1), (mine_b, 6), (swap_b, 7))
    ]

    kv = lax.all_to_all(kv_send, CTX, 0, 0, tiled=True)
    attended = attention(ctx_index[None].astype(jnp.int32), chunks, kv)
    attended_other = [lax.ppermute(a, "core", [(0, 1), (1, 0)]) for a in attended]
    partial_sums = project(core[None].astype(jnp.int32), attended, attended_other, first, second)
    parts = lax.all_to_all(partial_sums, EXP, 0, 0, tiled=True)
    positions = length // exp_count
    tokens = sequences * positions
    parts = parts.reshape(exp_count // quad_count, 2, 2, 2, positions, half)
    held = residual.reshape(positions, sequences, 2, half).transpose(2, 1, 0, 3)
    held = held.reshape(2, tokens, half)

    experts_all = w_gate.shape[0] * ctx_count * exp_count
    capacity = tokens * TOPK // experts_all
    dispatch, combine = routing(expert_ids, expert_gates, experts_all, capacity)
    outgoing, stream = norm_dispatch(parts, held, norm_gain.reshape(2, 1, half), dispatch)
    arrived = lax.all_to_all(
        outgoing.reshape(experts_all, 2 * capacity, half), ALL, 0, 0, tiled=True
    )
    produced = experts(
        arrived.reshape(experts_all * 2 * capacity, half), w_gate[0], w_up[0], w_down[0]
    )
    returned = lax.all_to_all(
        produced.reshape(experts_all, 2 * capacity, half), ALL, 0, 0, tiled=True
    )
    out = combine_rows(
        returned.reshape(experts_all * 2 * capacity, half), combine, stream
    )
    return out.reshape(residual.shape)


def solution(mesh):
    fine = Mesh(mesh.devices.reshape(SHAPE), ALL)
    rows = P(ALL, None, None)
    in_specs = (
        P(None, CTX, EXP),
        P(None, CTX, None),
        P(None, CTX, None),
        rows,
        P(EXP, None),
        P(),
        rows,
        rows,
        rows,
        rows,
        rows,
    )
    return jax.shard_map(local, mesh=fine, in_specs=in_specs, out_specs=rows, check_vma=False)
```

```python
import jax
import jax.numpy as jnp
from jax import lax
from jax.experimental import pallas as pl
from jax.experimental.pallas import tpu as pltpu
from jax.sharding import Mesh
from jax.sharding import PartitionSpec as P

HEAD = 128
TOPK = 8
CTX = ("x", "zl")
EXP = ("zh", "yh", "yl", "core")
ALL = CTX + EXP
QUAD = ("yl", "core")
SHAPE = (4, 2, 2, 2, 2, 2)
LOG2E = 1.4426950408889634
F32 = jnp.float32
BF16 = jnp.bfloat16
NEG = -1e30
CHUNKS = 6
VMEM = 40 * 1024 * 1024
VMEM_SMALL = 24 * 1024 * 1024


def cost(microseconds):
    return pl.CostEstimate(
        flops=int(microseconds * 1.1e9), bytes_accessed=1 << 20, transcendentals=0
    )


def nt(a, b):
    return lax.dot_general(a, b, (((1,), (1,)), ((), ())), preferred_element_type=F32)


def tn(a, b):
    return lax.dot_general(a, b, (((0,), (0,)), ((), ())), preferred_element_type=F32)


def attention_kernel(ctx_ref, *refs):
    q_hbm, kv_ref, out_refs = refs[:CHUNKS], refs[CHUNKS], refs[CHUNKS + 1 : CHUNKS + 3]
    q_refs, top_ref, sum_ref, acc_ref, sem = refs[CHUNKS + 3 :]
    loads = [pltpu.make_async_copy(q_hbm[c], q_refs.at[c], sem.at[c]) for c in range(CHUNKS)]
    for load in loads:
        load.start()
    for load in loads:
        load.wait()
    ctx = ctx_ref[0]
    length = kv_ref.shape[1]
    rows = 2 * length
    factor = HEAD**-0.5 * LOG2E

    def block(index, count, first):
        kv = kv_ref[pl.ds(index, count)].reshape(count * length, 2 * HEAD)
        key, value = kv[:, :HEAD], kv[:, HEAD:]
        for c in range(CHUNKS):
            query = jnp.concatenate([q_refs[c, :, :HEAD], q_refs[c, :, HEAD:]], axis=0)
            scores = nt(key, query)
            if first:
                shape = (count * length, rows)
                key_pos = lax.broadcasted_iota(jnp.int32, shape, 0) - (count - 1) * length
                query_pos = lax.broadcasted_iota(jnp.int32, shape, 1) % length
                scores = jnp.where(key_pos <= query_pos, scores, NEG)
            new = jnp.max(scores, axis=0, keepdims=True)
            if not first:
                old = top_ref[c]
                new = jnp.maximum(old, new)
            weights = jnp.exp2((scores - new) * factor)
            total = jnp.sum(weights, axis=0, keepdims=True)
            part = tn(value, weights.astype(BF16))
            if not first:
                shrink = jnp.exp2((old - new) * factor)
                total = total + sum_ref[c] * shrink
                part = part + acc_ref[c] * shrink
            sum_ref[c] = total
            acc_ref[c] = part
            top_ref[c] = new

    @pl.when(ctx % 2 == 1)
    def _():
        block(ctx - 1, 2, True)

    @pl.when(ctx % 2 == 0)
    def _():
        block(ctx, 1, True)

    @pl.loop(0, ctx // 2)
    def _(index):
        block(index * 2, 2, False)

    for c in range(CHUNKS):
        done = (acc_ref[c] / sum_ref[c]).T.astype(BF16)
        out_ref, start = out_refs[c % 2], c // 2 * 256
        out_ref[:, start : start + HEAD] = done[:length]
        out_ref[:, start + HEAD : start + 256] = done[length:]


def attention(ctx, chunks, kv):
    length = kv.shape[1]
    vmem = pl.BlockSpec(memory_space=pltpu.VMEM)
    return pl.pallas_call(
        attention_kernel,
        out_shape=(jax.ShapeDtypeStruct((length, 128 * CHUNKS), BF16),) * 2,
        in_specs=[pl.BlockSpec(memory_space=pltpu.SMEM)]
        + [pl.BlockSpec(memory_space=pl.ANY)] * CHUNKS
        + [vmem],
        out_specs=(vmem, vmem),
        scratch_shapes=[
            pltpu.VMEM((CHUNKS, length, 2 * HEAD), BF16),
            pltpu.VMEM((CHUNKS, 1, 2 * length), F32),
            pltpu.VMEM((CHUNKS, 1, 2 * length), F32),
            pltpu.VMEM((CHUNKS, HEAD, 2 * length), F32),
            pltpu.SemaphoreType.DMA((CHUNKS,)),
        ],
        compiler_params=pltpu.CompilerParams(vmem_limit_bytes=VMEM_SMALL),
        cost_estimate=cost(0.1),
        name="attention",
    )(ctx, *(pltpu.with_memory_space_constraint(q, pltpu.HBM) for q in chunks), kv)


def project_kernel(core_ref, own0_ref, own1_ref, other0_ref, other1_ref, *refs):
    first, second, out_ref = refs[:4], refs[4:8], refs[8]
    core = core_ref[0]
    length = own0_ref.shape[0]
    own_refs, other_refs = (own0_ref, own1_ref), (other0_ref, other1_ref)
    tile = out_ref.shape[3]
    steps = pl.num_programs(0)

    def run(parts):
        total = None
        for c, w_ref in parts:
            rows = jnp.concatenate(
                [
                    own_refs[c % 2][:, 256 * (c // 2) : 256 * (c // 2 + 1)],
                    other_refs[1 - c % 2][:, 256 * (c // 2) : 256 * (c // 2 + 1)],
                ],
                axis=0,
            )
            part = jnp.dot(rows, w_ref[...], preferred_element_type=F32)
            total = part if total is None else total + part
        total = total.astype(BF16)
        out_ref[:, core] = total[:length].reshape(-1, 16, tile)
        out_ref[:, 1 - core] = total[length:].reshape(-1, 16, tile)

    @pl.when(pl.program_id(0) < steps // 2)
    def _():
        run(zip((0, 1, 2, 3), first))

    @pl.when(pl.program_id(0) >= steps // 2)
    def _():
        run(zip((0, 1, 4, 5), second))


def project(core, own, other, first, second):
    rows, width = own[0].shape[0], first[0].shape[1]
    tile = 512
    steps = 2 * width // tile
    att = pl.BlockSpec(own[0].shape, lambda i: (0, 0))
    in_first = pl.BlockSpec((256, tile), lambda i: (0, jnp.minimum(i, steps // 2 - 1)))
    in_second = pl.BlockSpec((256, tile), lambda i: (0, jnp.maximum(i - steps // 2, 0)))
    return pl.pallas_call(
        project_kernel,
        grid=(steps,),
        out_shape=pltpu.HBM((rows // 16, 2, 16, 2 * width), BF16),
        in_specs=[pl.BlockSpec(memory_space=pltpu.SMEM)]
        + [att] * 4
        + [in_first] * 4
        + [in_second] * 4,
        out_specs=pl.BlockSpec((rows // 16, 2, 16, tile), lambda i: (0, 0, 0, i)),
        compiler_params=pltpu.CompilerParams(vmem_limit_bytes=VMEM_SMALL),
        cost_estimate=cost(0.1),
        name="project",
    )(core, *own, *other, *first, *second)


def norm_kernel(parts_ref, res_ref, gain_ref, dispatch_ref, out_ref, stream_ref, x_ref):
    groups, _, _, _, positions, half = parts_ref.shape
    squares = {}
    for s in range(4):
        rows = slice(positions * s, positions * (s + 1))
        total = None
        for h in range(2):
            value = res_ref[h, rows].astype(F32)
            for g in range(groups):
                value = value + parts_ref[g, s // 2, h, s % 2].astype(F32)
            value = value.astype(BF16)
            stream_ref[h, rows] = value
            value = value.astype(F32)
            part = jnp.sum(value * value, axis=1, keepdims=True)
            total = part if total is None else total + part
        squares[s] = lax.rsqrt(total / (2 * half) + 1e-06)
    for s in range(4):
        rows = slice(positions * s, positions * (s + 1))
        for h in range(2):
            value = stream_ref[h, rows].astype(F32) * squares[s] * gain_ref[h]
            x_ref[64 * h + positions * s : 64 * h + positions * (s + 1)] = value.astype(BF16)

    @pl.loop(0, half // 512)
    def _(i):
        cols = pl.ds(pl.multiple_of(i * 512, 512), 512)
        out_ref[:, cols] = jnp.dot(
            dispatch_ref[...], x_ref[:, cols], preferred_element_type=F32
        ).astype(BF16)


def norm_dispatch(parts, held, gain, dispatch):
    half = held.shape[2]
    vmem = pl.BlockSpec(memory_space=pltpu.VMEM)
    return pl.pallas_call(
        norm_kernel,
        out_shape=(
            jax.ShapeDtypeStruct((dispatch.shape[0], half), BF16),
            jax.ShapeDtypeStruct(held.shape, BF16),
        ),
        in_specs=[vmem] * 4,
        out_specs=(vmem, vmem),
        scratch_shapes=[pltpu.VMEM((dispatch.shape[1], half), BF16)],
        compiler_params=pltpu.CompilerParams(vmem_limit_bytes=VMEM_SMALL),
        cost_estimate=cost(2.2),
        name="norm_dispatch",
    )(parts, held, gain, dispatch)


def combine_kernel(ret_ref, combine_ref, stream_ref, out_ref):
    tile = ret_ref.shape[1]
    half = out_ref.shape[1] // 2
    tokens = out_ref.shape[0]
    step = pl.program_id(0)
    mixture = jnp.dot(combine_ref[...], ret_ref[...], preferred_element_type=F32)
    mixture = mixture[: 2 * tokens] + mixture[2 * tokens :]
    to = lax.broadcasted_iota(jnp.int32, (tokens, tokens), 0)
    frm = lax.broadcasted_iota(jnp.int32, (tokens, tokens), 1)
    order = jnp.where(frm == (to % 4) * (tokens // 4) + to // 4, 1.0, 0.0).astype(BF16)
    for h in range(2):
        back = jnp.dot(order, stream_ref[h], preferred_element_type=F32)
        cols = pl.ds(pl.multiple_of(h * half + step * tile, tile), tile)
        out_ref[:, cols] = (back + mixture[tokens * h : tokens * (h + 1)]).astype(BF16)


def combine_rows(returned, combine, stream):
    rows, half = returned.shape
    tokens = stream.shape[1]
    tile = 1024
    return pl.pallas_call(
        combine_kernel,
        grid=(half // tile,),
        out_shape=jax.ShapeDtypeStruct((tokens, 2 * half), BF16),
        in_specs=[
            pl.BlockSpec((rows, tile), lambda i: (0, i)),
            pl.BlockSpec(combine.shape, lambda i: (0, 0)),
            pl.BlockSpec((2, tokens, tile), lambda i: (0, 0, i)),
        ],
        out_specs=pl.BlockSpec((tokens, 2 * half), lambda i: (0, 0)),
        compiler_params=pltpu.CompilerParams(vmem_limit_bytes=VMEM_SMALL),
        cost_estimate=cost(4),
        name="combine",
    )(returned, combine, stream)


UP_TILE = 256
DOWN_TILE = 512
BLOCK = 256


def shuffle():
    r = lax.broadcasted_iota(jnp.int32, (BLOCK, BLOCK), 0)
    c = lax.broadcasted_iota(jnp.int32, (BLOCK, BLOCK), 1)
    half, r = r // 128, r % 128
    return jnp.where(c == (r // 4) * 8 + 4 * half + r % 4, 1.0, 0.0).astype(BF16)


def expert_kernel(
    r_ref, wg_hbm, wu_hbm, wd_hbm, out_hbm,
    x_ref, hid_ref, wg_ref, wu_ref, wd_ref, stage_ref, up_sem, down_sem, out_sem,
):
    rows, width = r_ref.shape
    ups = hid_ref.shape[1] // UP_TILE
    loads = []
    for i in range(ups):
        cols = slice(i * UP_TILE, (i + 1) * UP_TILE)
        loads.append(
            (
                pltpu.make_async_copy(wg_hbm.at[:, cols], wg_ref.at[i], up_sem.at[0, i]),
                pltpu.make_async_copy(wu_hbm.at[:, cols], wu_ref.at[i], up_sem.at[1, i]),
            )
        )
        for load in loads[-1]:
            load.start()
    load_down = pltpu.make_async_copy(wd_hbm, wd_ref, down_sem)
    load_down.start()
    matrix = shuffle()

    @pl.loop(0, rows // BLOCK)
    def _(b):
        block = r_ref[pl.ds(pl.multiple_of(b * BLOCK, BLOCK), BLOCK), :]
        moved = jnp.dot(matrix, block, preferred_element_type=F32).astype(BF16)
        to = pl.ds(pl.multiple_of(b * 128, 128), 128)
        x_ref[to, :width] = moved[:128]
        x_ref[to, width:] = moved[128:]

    for i in range(ups):
        for load in loads[i]:
            load.wait()
        x = x_ref[...]
        gate = jnp.dot(x, wg_ref[i], preferred_element_type=F32)
        up = jnp.dot(x, wu_ref[i], preferred_element_type=F32)
        hid_ref[:, i * UP_TILE : (i + 1) * UP_TILE] = (
            gate / (1.0 + jnp.exp(-gate)) * up
        ).astype(BF16)

    load_down.wait()
    stores = []
    for i in range(width // DOWN_TILE):
        cols = slice(i * DOWN_TILE, (i + 1) * DOWN_TILE)
        cols_high = slice(width + i * DOWN_TILE, width + (i + 1) * DOWN_TILE)
        hidden = hid_ref[...]
        low = jnp.dot(hidden, wd_ref[:, cols], preferred_element_type=F32).astype(BF16)
        high = jnp.dot(hidden, wd_ref[:, cols_high], preferred_element_type=F32).astype(BF16)
        for b in range(rows // BLOCK):
            part = slice(128 * b, 128 * (b + 1))
            both = jnp.concatenate([low[part], high[part]], axis=0)
            stage_ref[i, BLOCK * b : BLOCK * (b + 1), :] = tn(matrix, both).astype(BF16)
        store = pltpu.make_async_copy(stage_ref.at[i], out_hbm.at[:, cols], out_sem.at[i])
        store.start()
        stores.append(store)
    for store in stores:
        store.wait()


def experts(arrived, w_gate, w_up, w_down):
    rows, width = arrived.shape
    hidden = w_down.shape[0]
    ups, downs = hidden // UP_TILE, width // DOWN_TILE
    hbm = pl.BlockSpec(memory_space=pl.ANY)
    return pl.pallas_call(
        expert_kernel,
        out_shape=pltpu.HBM((rows, width), BF16),
        in_specs=[pl.BlockSpec(memory_space=pltpu.VMEM)] + [hbm] * 3,
        out_specs=hbm,
        scratch_shapes=[
            pltpu.VMEM((rows // 2, 2 * width), BF16),
            pltpu.VMEM((rows // 2, hidden), BF16),
            pltpu.VMEM((ups, 2 * width, UP_TILE), BF16),
            pltpu.VMEM((ups, 2 * width, UP_TILE), BF16),
            pltpu.VMEM(w_down.shape, BF16),
            pltpu.VMEM((downs, rows, DOWN_TILE), BF16),
            pltpu.SemaphoreType.DMA((2, ups)),
            pltpu.SemaphoreType.DMA,
            pltpu.SemaphoreType.DMA((downs,)),
        ],
        compiler_params=pltpu.CompilerParams(vmem_limit_bytes=VMEM),
        cost_estimate=cost(14),
        name="experts",
    )(
        pltpu.with_memory_space_constraint(arrived, pltpu.VMEM),
        *(pltpu.with_memory_space_constraint(w, pltpu.HBM) for w in (w_gate, w_up, w_down)),
    )


def routing(expert_ids, expert_gates, experts_all, capacity):
    positions, sequences, _ = expert_ids.shape
    tokens = positions * sequences
    flat_ids = expert_ids.reshape(-1)
    onehot = (flat_ids[:, None] == jnp.arange(experts_all, dtype=jnp.int32)[None, :]).astype(
        jnp.int32
    )
    before = jnp.cumsum(onehot, axis=0) - onehot
    slot = jnp.sum(before * onehot, axis=1)
    place = (flat_ids * 2 * capacity + slot).reshape(tokens, TOPK)
    rows = jnp.arange(2 * capacity * experts_all, dtype=jnp.int32)
    place_sp = place.reshape(positions, sequences, TOPK).transpose(1, 0, 2).reshape(tokens, TOPK)

    def dispatch_half(half):
        hit = rows[:, None, None] == place_sp[None] + half * capacity
        return jnp.any(hit, axis=2)

    dispatch = jnp.concatenate([dispatch_half(0), dispatch_half(1)], axis=1).astype(BF16)
    gates = expert_gates.reshape(tokens, TOPK)

    def combine_half(half):
        hit = rows[None, None, :] == (place + half * capacity)[:, :, None]
        return jnp.sum(jnp.where(hit, gates[:, :, None], 0.0), axis=1)

    combine = jnp.concatenate([combine_half(0), combine_half(1)], axis=0)
    high = combine.astype(BF16)
    low = (combine - high.astype(F32)).astype(BF16)
    return dispatch, jnp.concatenate([high, low], axis=0)


def local(
    queries,
    keys,
    values,
    residual,
    out_weight,
    norm_gain,
    expert_ids,
    expert_gates,
    w_gate,
    w_up,
    w_down,
):
    ctx_index = lax.axis_index(CTX)
    zh = lax.axis_index("zh")
    core = lax.axis_index("core")
    quad = lax.axis_index(QUAD)
    quad_count = lax.axis_size(QUAD)
    ctx_count = lax.axis_size(CTX)
    exp_count = lax.axis_size(EXP)
    sequences, length, _ = queries.shape
    width = residual.shape[2]

    def mine(a):
        a = lax.dynamic_index_in_dim(a, quad, 0, False)
        return lax.dynamic_slice_in_dim(a, zh * HEAD, HEAD, 1)

    kv_mine = jnp.concatenate([mine(keys), mine(values)], axis=1)
    kv_send = jnp.broadcast_to(kv_mine[None], (ctx_count,) + kv_mine.shape)

    half = width // 2
    part = half // 2
    ring = ("yh", "yl", "core")
    pairs = {m: [(i, i ^ m) for i in range(8)] for m in range(8)}
    chunks = [lax.dynamic_index_in_dim(queries, quad, 0, False)]
    for m in (1, 2, 3, 6, 7):
        chunk = lax.dynamic_index_in_dim(queries, quad ^ (m & 3), 0, False)
        chunks.append(lax.ppermute(chunk, ring, pairs[m]))

    def columns(of_core, second):
        start = of_core * half + (part if second else 0)
        return lax.dynamic_slice_in_dim(out_weight, start, part, 1)

    mine_a, mine_b, swap_a, swap_b, _ = lax.optimization_barrier(
        (
            columns(core, False),
            columns(core, True),
            columns(1 - core, False),
            columns(1 - core, True),
            chunks[1:],
        )
    )
    first = [mine_a] + [
        lax.ppermute(w, ring, pairs[m]) for w, m in ((swap_a, 1), (mine_a, 2), (swap_a, 3))
    ]
    second = [mine_b] + [
        lax.ppermute(w, ring, pairs[m]) for w, m in ((swap_b, 1), (mine_b, 6), (swap_b, 7))
    ]

    kv = lax.all_to_all(kv_send, CTX, 0, 0, tiled=True)
    attended = attention(ctx_index[None].astype(jnp.int32), chunks, kv)
    attended_other = [lax.ppermute(a, "core", [(0, 1), (1, 0)]) for a in attended]
    partial_sums = project(core[None].astype(jnp.int32), attended, attended_other, first, second)
    parts = lax.all_to_all(partial_sums, EXP, 0, 0, tiled=True)
    positions = length // exp_count
    tokens = sequences * positions
    parts = parts.reshape(exp_count // quad_count, 2, 2, 2, positions, half)
    held = residual.reshape(positions, sequences, 2, half).transpose(2, 1, 0, 3)
    held = held.reshape(2, tokens, half)

    experts_all = w_gate.shape[0] * ctx_count * exp_count
    capacity = tokens * TOPK // experts_all
    dispatch, combine = routing(expert_ids, expert_gates, experts_all, capacity)
    outgoing, stream = norm_dispatch(parts, held, norm_gain.reshape(2, 1, half), dispatch)
    arrived = lax.all_to_all(
        outgoing.reshape(experts_all, 2 * capacity, half), ALL, 0, 0, tiled=True
    )
    produced = experts(
        arrived.reshape(experts_all * 2 * capacity, half), w_gate[0], w_up[0], w_down[0]
    )
    returned = lax.all_to_all(
        produced.reshape(experts_all, 2 * capacity, half), ALL, 0, 0, tiled=True
    )
    out = combine_rows(
        returned.reshape(experts_all * 2 * capacity, half), combine, stream
    )
    return out.reshape(residual.shape)


def solution(mesh):
    fine = Mesh(mesh.devices.reshape(SHAPE), ALL)
    rows = P(ALL, None, None)
    in_specs = (
        P(None, CTX, EXP),
        P(None, CTX, None),
        P(None, CTX, None),
        rows,
        P(EXP, None),
        P(),
        rows,
        rows,
        rows,
        rows,
        rows,
    )
    return jax.shard_map(local, mesh=fine, in_specs=in_specs, out_specs=rows, check_vma=False)
```

```python
import jax
import jax.numpy as jnp
from jax import lax
from jax.experimental import pallas as pl
from jax.experimental.pallas import tpu as pltpu
from jax.sharding import Mesh
from jax.sharding import PartitionSpec as P

HEAD = 128
TOPK = 8
CTX = ("x", "zl")
EXP = ("zh", "yh", "yl", "core")
ALL = CTX + EXP
QUAD = ("yl", "core")
SHAPE = (4, 2, 2, 2, 2, 2)
LOG2E = 1.4426950408889634
F32 = jnp.float32
BF16 = jnp.bfloat16
NEG = -1e30
CHUNKS = 6
VMEM = 40 * 1024 * 1024
VMEM_SMALL = 24 * 1024 * 1024


def cost(microseconds):
    return pl.CostEstimate(
        flops=int(microseconds * 1.1e9), bytes_accessed=1 << 20, transcendentals=0
    )


def nt(a, b):
    return lax.dot_general(a, b, (((1,), (1,)), ((), ())), preferred_element_type=F32)


def tn(a, b):
    return lax.dot_general(a, b, (((0,), (0,)), ((), ())), preferred_element_type=F32)


def attention_kernel(ctx_ref, *refs):
    q_hbm, kv_ref, out_refs = refs[:CHUNKS], refs[CHUNKS], refs[CHUNKS + 1 : CHUNKS + 3]
    q_refs, top_ref, sum_ref, acc_ref, sem = refs[CHUNKS + 3 :]
    loads = [pltpu.make_async_copy(q_hbm[c], q_refs.at[c], sem.at[c]) for c in range(CHUNKS)]
    for load in loads:
        load.start()
    for load in loads:
        load.wait()
    ctx = ctx_ref[0]
    length = kv_ref.shape[1]
    rows = 2 * length
    factor = HEAD**-0.5 * LOG2E

    def block(index, count, first):
        kv = kv_ref[pl.ds(index, count)].reshape(count * length, 2 * HEAD)
        key, value = kv[:, :HEAD], kv[:, HEAD:]
        for c in range(CHUNKS):
            query = jnp.concatenate([q_refs[c, :, :HEAD], q_refs[c, :, HEAD:]], axis=0)
            scores = nt(key, query)
            if first:
                shape = (count * length, rows)
                key_pos = lax.broadcasted_iota(jnp.int32, shape, 0) - (count - 1) * length
                query_pos = lax.broadcasted_iota(jnp.int32, shape, 1) % length
                scores = jnp.where(key_pos <= query_pos, scores, NEG)
            new = jnp.max(scores, axis=0, keepdims=True)
            if not first:
                old = top_ref[c]
                new = jnp.maximum(old, new)
            weights = jnp.exp2((scores - new) * factor)
            total = jnp.sum(weights, axis=0, keepdims=True)
            part = tn(value, weights.astype(BF16))
            if not first:
                shrink = jnp.exp2((old - new) * factor)
                total = total + sum_ref[c] * shrink
                part = part + acc_ref[c] * shrink
            sum_ref[c] = total
            acc_ref[c] = part
            top_ref[c] = new

    @pl.when(ctx % 2 == 1)
    def _():
        block(ctx - 1, 2, True)

    @pl.when(ctx % 2 == 0)
    def _():
        block(ctx, 1, True)

    @pl.loop(0, ctx // 2)
    def _(index):
        block(index * 2, 2, False)

    for c in range(CHUNKS):
        done = (acc_ref[c] / sum_ref[c]).T.astype(BF16)
        out_ref, start = out_refs[c % 2], c // 2 * 256
        out_ref[:, start : start + HEAD] = done[:length]
        out_ref[:, start + HEAD : start + 256] = done[length:]


def attention(ctx, chunks, kv):
    length = kv.shape[1]
    vmem = pl.BlockSpec(memory_space=pltpu.VMEM)
    return pl.pallas_call(
        attention_kernel,
        out_shape=(jax.ShapeDtypeStruct((length, 128 * CHUNKS), BF16),) * 2,
        in_specs=[pl.BlockSpec(memory_space=pltpu.SMEM)]
        + [pl.BlockSpec(memory_space=pl.ANY)] * CHUNKS
        + [vmem],
        out_specs=(vmem, vmem),
        scratch_shapes=[
            pltpu.VMEM((CHUNKS, length, 2 * HEAD), BF16),
            pltpu.VMEM((CHUNKS, 1, 2 * length), F32),
            pltpu.VMEM((CHUNKS, 1, 2 * length), F32),
            pltpu.VMEM((CHUNKS, HEAD, 2 * length), F32),
            pltpu.SemaphoreType.DMA((CHUNKS,)),
        ],
        compiler_params=pltpu.CompilerParams(vmem_limit_bytes=VMEM_SMALL),
        cost_estimate=cost(0.1),
        name="attention",
    )(ctx, *(pltpu.with_memory_space_constraint(q, pltpu.HBM) for q in chunks), kv)


def project_kernel(core_ref, own0_ref, own1_ref, other0_ref, other1_ref, *refs):
    first, second, out_ref = refs[:4], refs[4:8], refs[8]
    core = core_ref[0]
    length = own0_ref.shape[0]
    own_refs, other_refs = (own0_ref, own1_ref), (other0_ref, other1_ref)
    tile = out_ref.shape[3]
    steps = pl.num_programs(0)

    def run(parts):
        total = None
        for c, w_ref in parts:
            rows = jnp.concatenate(
                [
                    own_refs[c % 2][:, 256 * (c // 2) : 256 * (c // 2 + 1)],
                    other_refs[1 - c % 2][:, 256 * (c // 2) : 256 * (c // 2 + 1)],
                ],
                axis=0,
            )
            part = jnp.dot(rows, w_ref[...], preferred_element_type=F32)
            total = part if total is None else total + part
        total = total.astype(BF16)
        out_ref[:, core] = total[:length].reshape(-1, 16, tile)
        out_ref[:, 1 - core] = total[length:].reshape(-1, 16, tile)

    @pl.when(pl.program_id(0) < steps // 2)
    def _():
        run(zip((0, 1, 2, 3), first))

    @pl.when(pl.program_id(0) >= steps // 2)
    def _():
        run(zip((0, 1, 4, 5), second))


def project(core, own, other, first, second):
    rows, width = own[0].shape[0], first[0].shape[1]
    tile = 1024
    steps = 2 * width // tile
    att = pl.BlockSpec(own[0].shape, lambda i: (0, 0))
    in_first = pl.BlockSpec((256, tile), lambda i: (0, jnp.minimum(i, steps // 2 - 1)))
    in_second = pl.BlockSpec((256, tile), lambda i: (0, jnp.maximum(i - steps // 2, 0)))
    return pl.pallas_call(
        project_kernel,
        grid=(steps,),
        out_shape=pltpu.HBM((rows // 16, 2, 16, 2 * width), BF16),
        in_specs=[pl.BlockSpec(memory_space=pltpu.SMEM)]
        + [att] * 4
        + [in_first] * 4
        + [in_second] * 4,
        out_specs=pl.BlockSpec((rows // 16, 2, 16, tile), lambda i: (0, 0, 0, i)),
        compiler_params=pltpu.CompilerParams(vmem_limit_bytes=VMEM_SMALL),
        cost_estimate=cost(0.1),
        name="project",
    )(core, *own, *other, *first, *second)


def norm_kernel(parts_ref, res_ref, gain_ref, dispatch_ref, out_ref, stream_ref, x_ref):
    groups, _, _, _, positions, half = parts_ref.shape
    squares = {}
    for s in range(4):
        rows = slice(positions * s, positions * (s + 1))
        total = None
        for h in range(2):
            value = res_ref[h, rows].astype(F32)
            for g in range(groups):
                value = value + parts_ref[g, s // 2, h, s % 2].astype(F32)
            value = value.astype(BF16)
            stream_ref[h, rows] = value
            value = value.astype(F32)
            part = jnp.sum(value * value, axis=1, keepdims=True)
            total = part if total is None else total + part
        squares[s] = lax.rsqrt(total / (2 * half) + 1e-06)
    for s in range(4):
        rows = slice(positions * s, positions * (s + 1))
        for h in range(2):
            value = stream_ref[h, rows].astype(F32) * squares[s] * gain_ref[h]
            x_ref[64 * h + positions * s : 64 * h + positions * (s + 1)] = value.astype(BF16)

    @pl.loop(0, half // 512)
    def _(i):
        cols = pl.ds(pl.multiple_of(i * 512, 512), 512)
        out_ref[:, cols] = jnp.dot(
            dispatch_ref[...], x_ref[:, cols], preferred_element_type=F32
        ).astype(BF16)


def norm_dispatch(parts, held, gain, dispatch):
    half = held.shape[2]
    vmem = pl.BlockSpec(memory_space=pltpu.VMEM)
    return pl.pallas_call(
        norm_kernel,
        out_shape=(
            jax.ShapeDtypeStruct((dispatch.shape[0], half), BF16),
            jax.ShapeDtypeStruct(held.shape, BF16),
        ),
        in_specs=[vmem] * 4,
        out_specs=(vmem, vmem),
        scratch_shapes=[pltpu.VMEM((dispatch.shape[1], half), BF16)],
        compiler_params=pltpu.CompilerParams(vmem_limit_bytes=VMEM_SMALL),
        cost_estimate=cost(2.2),
        name="norm_dispatch",
    )(parts, held, gain, dispatch)


def combine_kernel(ret_ref, combine_ref, stream_ref, out_ref):
    tile = ret_ref.shape[1]
    half = out_ref.shape[1] // 2
    tokens = out_ref.shape[0]
    step = pl.program_id(0)
    mixture = jnp.dot(combine_ref[...], ret_ref[...], preferred_element_type=F32)
    mixture = mixture[: 2 * tokens] + mixture[2 * tokens :]
    to = lax.broadcasted_iota(jnp.int32, (tokens, tokens), 0)
    frm = lax.broadcasted_iota(jnp.int32, (tokens, tokens), 1)
    order = jnp.where(frm == (to % 4) * (tokens // 4) + to // 4, 1.0, 0.0).astype(BF16)
    for h in range(2):
        back = jnp.dot(order, stream_ref[h], preferred_element_type=F32)
        cols = pl.ds(pl.multiple_of(h * half + step * tile, tile), tile)
        out_ref[:, cols] = (back + mixture[tokens * h : tokens * (h + 1)]).astype(BF16)


def combine_rows(returned, combine, stream):
    rows, half = returned.shape
    tokens = stream.shape[1]
    tile = 1024
    return pl.pallas_call(
        combine_kernel,
        grid=(half // tile,),
        out_shape=jax.ShapeDtypeStruct((tokens, 2 * half), BF16),
        in_specs=[
            pl.BlockSpec((rows, tile), lambda i: (0, i)),
            pl.BlockSpec(combine.shape, lambda i: (0, 0)),
            pl.BlockSpec((2, tokens, tile), lambda i: (0, 0, i)),
        ],
        out_specs=pl.BlockSpec((tokens, 2 * half), lambda i: (0, 0)),
        compiler_params=pltpu.CompilerParams(vmem_limit_bytes=VMEM_SMALL),
        cost_estimate=cost(4),
        name="combine",
    )(returned, combine, stream)


UP_TILE = 256
DOWN_TILE = 512
BLOCK = 256


def shuffle():
    r = lax.broadcasted_iota(jnp.int32, (BLOCK, BLOCK), 0)
    c = lax.broadcasted_iota(jnp.int32, (BLOCK, BLOCK), 1)
    half, r = r // 128, r % 128
    return jnp.where(c == (r // 4) * 8 + 4 * half + r % 4, 1.0, 0.0).astype(BF16)


def expert_kernel(
    r_ref, wg_hbm, wu_hbm, wd_hbm, out_hbm,
    x_ref, hid_ref, wg_ref, wu_ref, wd_ref, stage_ref, up_sem, down_sem, out_sem,
):
    rows, width = r_ref.shape
    ups = hid_ref.shape[1] // UP_TILE
    loads = []
    for i in range(ups):
        cols = slice(i * UP_TILE, (i + 1) * UP_TILE)
        loads.append(
            (
                pltpu.make_async_copy(wg_hbm.at[:, cols], wg_ref.at[i], up_sem.at[0, i]),
                pltpu.make_async_copy(wu_hbm.at[:, cols], wu_ref.at[i], up_sem.at[1, i]),
            )
        )
        for load in loads[-1]:
            load.start()
    load_down = pltpu.make_async_copy(wd_hbm, wd_ref, down_sem)
    load_down.start()
    matrix = shuffle()

    @pl.loop(0, rows // BLOCK)
    def _(b):
        block = r_ref[pl.ds(pl.multiple_of(b * BLOCK, BLOCK), BLOCK), :]
        moved = jnp.dot(matrix, block, preferred_element_type=F32).astype(BF16)
        to = pl.ds(pl.multiple_of(b * 128, 128), 128)
        x_ref[to, :width] = moved[:128]
        x_ref[to, width:] = moved[128:]

    for i in range(ups):
        for load in loads[i]:
            load.wait()
        x = x_ref[...]
        gate = jnp.dot(x, wg_ref[i], preferred_element_type=F32)
        up = jnp.dot(x, wu_ref[i], preferred_element_type=F32)
        hid_ref[:, i * UP_TILE : (i + 1) * UP_TILE] = (
            gate / (1.0 + jnp.exp(-gate)) * up
        ).astype(BF16)

    load_down.wait()
    stores = []
    for i in range(width // DOWN_TILE):
        cols = slice(i * DOWN_TILE, (i + 1) * DOWN_TILE)
        cols_high = slice(width + i * DOWN_TILE, width + (i + 1) * DOWN_TILE)
        hidden = hid_ref[...]
        low = jnp.dot(hidden, wd_ref[:, cols], preferred_element_type=F32).astype(BF16)
        high = jnp.dot(hidden, wd_ref[:, cols_high], preferred_element_type=F32).astype(BF16)
        for b in range(rows // BLOCK):
            part = slice(128 * b, 128 * (b + 1))
            both = jnp.concatenate([low[part], high[part]], axis=0)
            stage_ref[i, BLOCK * b : BLOCK * (b + 1), :] = tn(matrix, both).astype(BF16)
        store = pltpu.make_async_copy(stage_ref.at[i], out_hbm.at[:, cols], out_sem.at[i])
        store.start()
        stores.append(store)
    for store in stores:
        store.wait()


def experts(arrived, w_gate, w_up, w_down):
    rows, width = arrived.shape
    hidden = w_down.shape[0]
    ups, downs = hidden // UP_TILE, width // DOWN_TILE
    hbm = pl.BlockSpec(memory_space=pl.ANY)
    return pl.pallas_call(
        expert_kernel,
        out_shape=pltpu.HBM((rows, width), BF16),
        in_specs=[pl.BlockSpec(memory_space=pltpu.VMEM)] + [hbm] * 3,
        out_specs=hbm,
        scratch_shapes=[
            pltpu.VMEM((rows // 2, 2 * width), BF16),
            pltpu.VMEM((rows // 2, hidden), BF16),
            pltpu.VMEM((ups, 2 * width, UP_TILE), BF16),
            pltpu.VMEM((ups, 2 * width, UP_TILE), BF16),
            pltpu.VMEM(w_down.shape, BF16),
            pltpu.VMEM((downs, rows, DOWN_TILE), BF16),
            pltpu.SemaphoreType.DMA((2, ups)),
            pltpu.SemaphoreType.DMA,
            pltpu.SemaphoreType.DMA((downs,)),
        ],
        compiler_params=pltpu.CompilerParams(vmem_limit_bytes=VMEM),
        cost_estimate=cost(14),
        name="experts",
    )(
        pltpu.with_memory_space_constraint(arrived, pltpu.VMEM),
        *(pltpu.with_memory_space_constraint(w, pltpu.HBM) for w in (w_gate, w_up, w_down)),
    )


def routing(expert_ids, expert_gates, experts_all, capacity):
    positions, sequences, _ = expert_ids.shape
    tokens = positions * sequences
    flat_ids = expert_ids.reshape(-1)
    onehot = (flat_ids[:, None] == jnp.arange(experts_all, dtype=jnp.int32)[None, :]).astype(
        jnp.int32
    )
    before = jnp.cumsum(onehot, axis=0) - onehot
    slot = jnp.sum(before * onehot, axis=1)
    place = (flat_ids * 2 * capacity + slot).reshape(tokens, TOPK)
    rows = jnp.arange(2 * capacity * experts_all, dtype=jnp.int32)
    place_sp = place.reshape(positions, sequences, TOPK).transpose(1, 0, 2).reshape(tokens, TOPK)

    def dispatch_half(half):
        hit = rows[:, None, None] == place_sp[None] + half * capacity
        return jnp.any(hit, axis=2)

    dispatch = jnp.concatenate([dispatch_half(0), dispatch_half(1)], axis=1).astype(BF16)
    gates = expert_gates.reshape(tokens, TOPK)

    def combine_half(half):
        hit = rows[None, None, :] == (place + half * capacity)[:, :, None]
        return jnp.sum(jnp.where(hit, gates[:, :, None], 0.0), axis=1)

    combine = jnp.concatenate([combine_half(0), combine_half(1)], axis=0)
    high = combine.astype(BF16)
    low = (combine - high.astype(F32)).astype(BF16)
    return dispatch, jnp.concatenate([high, low], axis=0)


def local(
    queries,
    keys,
    values,
    residual,
    out_weight,
    norm_gain,
    expert_ids,
    expert_gates,
    w_gate,
    w_up,
    w_down,
):
    ctx_index = lax.axis_index(CTX)
    zh = lax.axis_index("zh")
    core = lax.axis_index("core")
    quad = lax.axis_index(QUAD)
    quad_count = lax.axis_size(QUAD)
    ctx_count = lax.axis_size(CTX)
    exp_count = lax.axis_size(EXP)
    sequences, length, _ = queries.shape
    width = residual.shape[2]

    def mine(a):
        a = lax.dynamic_index_in_dim(a, quad, 0, False)
        return lax.dynamic_slice_in_dim(a, zh * HEAD, HEAD, 1)

    kv_mine = jnp.concatenate([mine(keys), mine(values)], axis=1)
    kv_send = jnp.broadcast_to(kv_mine[None], (ctx_count,) + kv_mine.shape)

    half = width // 2
    part = half // 2
    ring = ("yh", "yl", "core")
    pairs = {m: [(i, i ^ m) for i in range(8)] for m in range(8)}
    chunks = [lax.dynamic_index_in_dim(queries, quad, 0, False)]
    for m in (1, 2, 3, 6, 7):
        chunk = lax.dynamic_index_in_dim(queries, quad ^ (m & 3), 0, False)
        chunks.append(lax.ppermute(chunk, ring, pairs[m]))

    def columns(of_core, second):
        start = of_core * half + (part if second else 0)
        return lax.dynamic_slice_in_dim(out_weight, start, part, 1)

    mine_a, mine_b, swap_a, swap_b, _ = lax.optimization_barrier(
        (
            columns(core, False),
            columns(core, True),
            columns(1 - core, False),
            columns(1 - core, True),
            chunks[1:],
        )
    )
    first = [mine_a] + [
        lax.ppermute(w, ring, pairs[m]) for w, m in ((swap_a, 1), (mine_a, 2), (swap_a, 3))
    ]
    second = [mine_b] + [
        lax.ppermute(w, ring, pairs[m]) for w, m in ((swap_b, 1), (mine_b, 6), (swap_b, 7))
    ]

    kv = lax.all_to_all(kv_send, CTX, 0, 0, tiled=True)
    attended = attention(ctx_index[None].astype(jnp.int32), chunks, kv)
    attended_other = [lax.ppermute(a, "core", [(0, 1), (1, 0)]) for a in attended]
    partial_sums = project(core[None].astype(jnp.int32), attended, attended_other, first, second)
    parts = lax.all_to_all(partial_sums, EXP, 0, 0, tiled=True)
    positions = length // exp_count
    tokens = sequences * positions
    parts = parts.reshape(exp_count // quad_count, 2, 2, 2, positions, half)
    held = residual.reshape(positions, sequences, 2, half).transpose(2, 1, 0, 3)
    held = held.reshape(2, tokens, half)

    experts_all = w_gate.shape[0] * ctx_count * exp_count
    capacity = tokens * TOPK // experts_all
    dispatch, combine = routing(expert_ids, expert_gates, experts_all, capacity)
    outgoing, stream = norm_dispatch(parts, held, norm_gain.reshape(2, 1, half), dispatch)
    arrived = lax.all_to_all(
        outgoing.reshape(experts_all, 2 * capacity, half), ALL, 0, 0, tiled=True
    )
    produced = experts(
        arrived.reshape(experts_all * 2 * capacity, half), w_gate[0], w_up[0], w_down[0]
    )
    returned = lax.all_to_all(
        produced.reshape(experts_all, 2 * capacity, half), ALL, 0, 0, tiled=True
    )
    out = combine_rows(
        returned.reshape(experts_all * 2 * capacity, half), combine, stream
    )
    return out.reshape(residual.shape)


def solution(mesh):
    fine = Mesh(mesh.devices.reshape(SHAPE), ALL)
    rows = P(ALL, None, None)
    in_specs = (
        P(None, CTX, EXP),
        P(None, CTX, None),
        P(None, CTX, None),
        rows,
        P(EXP, None),
        P(),
        rows,
        rows,
        rows,
        rows,
        rows,
    )
    return jax.shard_map(local, mesh=fine, in_specs=in_specs, out_specs=rows, check_vma=False)
```
